256 devices in a mesh: beam: 32 (over y, x, core), mp: 8 (over z).
Axes of the slice: x: 4, y: 4, z: 8, core: 2. Of those that a mesh axis runs over, the one named last changes fastest.
Arguments:
- queries: bfloat16 [512, 128, 8192], P('beam', None, 'mp'), may hold values from -10 to 10
- new_kv: bfloat16 [512, 2, 128, 1024], P('beam', None, None, 'mp'), may hold values from -6 to 6
- newest_key_value: bfloat16 [512, 2, 128, 1024], P('beam', None, None, 'mp'), may hold values from -6 to 6
- ancestor_block_store: bfloat16 [384, 2, 128, 1024], P('beam', None, None, 'mp'), may hold values from -6 to 6
- parent: int32 [512], replicated, may hold values from 0 to 511, as said below
- ancestors: int32 [512, 5], P('beam'), may hold values from 0 to 383, as said below
- ancestor_count: int32 [512], P('beam'), may hold values from 1 to 5, as said below
- keep_list: int32 [256], replicated, may hold values from 0 to 511, as said below
- w_reward: bfloat16 [8192], P('mp'), may hold values from -0.0625 to 0.0625
Outputs:
- reward: float32 [512, 128], P('beam')
- kept_blocks: bfloat16 [256, 2, 128, 1024], P('beam', None, None, 'mp')
The draws below stay inside these ranges and needn't reach their ends.
Inputs may be any that keep to these rules, and one draw needn't show every extreme that they name: Each parent has exactly 2 children, consecutive beams of one device starting at a multiple of 2. The groups of children on one device have parents on distinct devices if there are at most as many groups on a device as devices; otherwise at most 2 groups share a parent device, and on every device some 2 do. `keep_list`: distinct beams; survivor j goes to device j // 8. The survivors bound for one device come from distinct devices if there are at most as many of them as devices; otherwise at most 2 come from one device, and on every device some 2 do. `ancestors`: 5 distinct blocks per beam, all among the 12 pool blocks held by the beam's own device. `ancestor_count`: every device has a beam with all 5 slots live.
All inputs are finite; a program needn't handle non-finite values.
Results may differ from the reference program's by a relative error of at most 0.0049.
Values may be sent and summed in bfloat16 or wider, within the bound.
A program may use at most 64 MiB of HBM per device.

```python
import jax
import jax.numpy as jnp
import numpy as np
from jax import lax

QUERY_HEADS = 64
KEY_VALUE_HEADS = 8
HEAD_SIZE = 128
BLOCK_TOKENS = 128
CHILD = 2
ANC = 5
ANCESTOR_BLOCKS = 12
BEAM_DEV = 16
BEAM_TOTAL = 512
N_BEAM = 32


def source_table(key, salt):
    groups_dev = BEAM_DEV // CHILD
    paired = max(0, groups_dev - N_BEAM)
    random_base_key = jax.random.fold_in(key, salt)
    offset_perm = jax.random.permutation(jax.random.fold_in(random_base_key, 1), N_BEAM)
    outer_perm = jax.random.permutation(jax.random.fold_in(random_base_key, 2), N_BEAM)
    inner_perm = jax.random.permutation(jax.random.fold_in(random_base_key, 3), N_BEAM)
    index_table = jnp.array(np.array([g // 2 if g < 2 * paired else g - paired for g in range(groups_dev)], dtype=np.int32))
    offsets = offset_perm[index_table]
    sources = outer_perm[(inner_perm[:, None] + offsets[None, :]) % N_BEAM]
    within = jax.random.randint(jax.random.fold_in(random_base_key, 4), (N_BEAM, groups_dev), 0, CHILD)
    chosen = sources * BEAM_DEV + jnp.arange(groups_dev)[None, :] * CHILD + within
    ranking = jax.random.randint(jax.random.fold_in(random_base_key, 5), (N_BEAM, groups_dev), 0, 1 << 20) * groups_dev + jnp.arange(groups_dev)[None, :]
    ordering = jnp.argsort(ranking, axis=1)
    return jnp.take_along_axis(chosen, ordering, axis=1).astype(jnp.int32)


def draw_parent(key, part):
    return jnp.repeat(source_table(key, 17).reshape(-1), CHILD).astype(jnp.int32)


def draw_keep_list(key, part):
    return source_table(key, 29).reshape(-1).astype(jnp.int32)


def draw_ancestors(key, part):
    ranking = jax.random.randint(jax.random.fold_in(key, 31), (BEAM_TOTAL, ANCESTOR_BLOCKS), 0, 1 << 20) * ANCESTOR_BLOCKS + jnp.arange(ANCESTOR_BLOCKS)[None, :]
    local_ids = jnp.argsort(ranking, axis=1)[:, :ANC]
    return (local_ids + (jnp.arange(BEAM_TOTAL) // BEAM_DEV)[:, None] * ANCESTOR_BLOCKS).astype(jnp.int32)


def draw_ancestor_count(key, part):
    lengths = jax.random.randint(jax.random.fold_in(key, 37), (BEAM_TOTAL,), 1, ANC + 1)
    full_at = jax.random.randint(jax.random.fold_in(key, 38), (N_BEAM,), 0, BEAM_DEV)
    position = jnp.arange(BEAM_TOTAL) % BEAM_DEV
    device_of = jnp.arange(BEAM_TOTAL) // BEAM_DEV
    return jnp.where(position == full_at[device_of], ANC, lengths).astype(jnp.int32)


def draw_queries(key, part):
    random_base_key = jax.random.fold_in(key, 41)
    value_entries = 2.5 * jax.random.truncated_normal(jax.random.fold_in(random_base_key, 1), -4.0, 4.0, (BEAM_TOTAL, BLOCK_TOKENS, QUERY_HEADS * HEAD_SIZE), jnp.float32)
    return value_entries.astype(jnp.bfloat16)


def draw_new_kv(key, part):
    random_base_key = jax.random.fold_in(key, 53)
    value_entries = jax.random.truncated_normal(jax.random.fold_in(random_base_key, 1), -6.0, 6.0, (BEAM_TOTAL, 2, BLOCK_TOKENS, KEY_VALUE_HEADS * HEAD_SIZE), jnp.float32)
    return value_entries.astype(jnp.bfloat16)


def steps_of(own_key, shape, cuts, low, high):
    loudness = 1.0
    for dim, parts in cuts:
        heights = jax.random.uniform(jax.random.fold_in(jax.random.fold_in(own_key, 6), dim), (parts,), jnp.float32, low / len(cuts), high / len(cuts))
        loudness = loudness * jnp.repeat(jnp.exp(heights), shape[dim] // parts).reshape((-1,) + (1,) * (len(shape) - 1 - dim))
    return loudness


def gaussian(own_key, dims, scale, reach, split=(), kind=jnp.bfloat16):
    drawn = jax.random.normal(own_key, dims, jnp.float32) * scale
    if len(split) > 0:
        drawn = steps_of(own_key, dims, split, -0.22, 0.18) * drawn
    return jnp.clip(drawn, min=-reach, max=reach).astype(kind)


def setup_inputs(seed: int = 0) -> dict:
    key_list = jax.random.split(jax.random.key(seed), 10)
    queries = draw_queries(jax.random.fold_in(key_list[9], 71), 0)
    new_kv = draw_new_kv(jax.random.fold_in(key_list[9], 71), 0)
    newest_key_value = gaussian(key_list[2], (BEAM_TOTAL, 2, BLOCK_TOKENS, KEY_VALUE_HEADS * HEAD_SIZE), 1.0, 6.0, ((0, 32), (3, 8)))
    ancestor_block_store = gaussian(key_list[3], (N_BEAM * ANCESTOR_BLOCKS, 2, BLOCK_TOKENS, KEY_VALUE_HEADS * HEAD_SIZE), 1.0, 6.0, ((0, 32), (3, 8)))
    parent = draw_parent(jax.random.fold_in(key_list[9], 71), 0)
    ancestors = draw_ancestors(jax.random.fold_in(key_list[9], 71), 0)
    ancestor_count = draw_ancestor_count(jax.random.fold_in(key_list[9], 71), 0)
    keep_list = draw_keep_list(jax.random.fold_in(key_list[9], 71), 0)
    w_reward = gaussian(key_list[8], (QUERY_HEADS * HEAD_SIZE,), (QUERY_HEADS * HEAD_SIZE) ** -0.5, 0.0625, ((0, 8),))
    return dict(queries=queries, new_kv=new_kv, newest_key_value=newest_key_value, ancestor_block_store=ancestor_block_store, parent=parent, ancestors=ancestors, ancestor_count=ancestor_count, keep_list=keep_list, w_reward=w_reward)


def reference(queries, new_kv, newest_key_value, ancestor_block_store, parent, ancestors, ancestor_count, keep_list, w_reward):
    scale_factor = HEAD_SIZE ** -0.5
    query_groups_per_head = QUERY_HEADS // KEY_VALUE_HEADS
    total_key_count = (ANC + 2) * BLOCK_TOKENS
    key_slot = jnp.arange(total_key_count) // BLOCK_TOKENS
    key_pos = jnp.arange(total_key_count) % BLOCK_TOKENS
    tok_pos = jnp.arange(BLOCK_TOKENS)
    parent_kv = jnp.take(newest_key_value, parent, axis=0)

    def attend_beam(pieces):
        current_query_block, own_block, parent_block, block_ids, live_count = pieces
        block_list = jnp.concatenate([jnp.take(ancestor_block_store, block_ids, axis=0), parent_block[None], own_block[None]], axis=0)
        key_row_matrix = block_list[:, 0].reshape(total_key_count, KEY_VALUE_HEADS, HEAD_SIZE).astype(jnp.float32)
        value_row_matrix = block_list[:, 1].reshape(total_key_count, KEY_VALUE_HEADS, HEAD_SIZE).astype(jnp.float32)
        query_row_matrix = current_query_block.reshape(BLOCK_TOKENS, KEY_VALUE_HEADS, query_groups_per_head, HEAD_SIZE).astype(jnp.float32)
        scores = jnp.einsum("tkgd,jkd->kgtj", query_row_matrix, key_row_matrix) * scale_factor
        allowed = jnp.where((key_slot < ANC)[None, :], (key_slot < live_count)[None, :],
                            jnp.where((key_slot == ANC)[None, :], True, key_pos[None, :] <= tok_pos[:, None]))
        scores = jnp.where(allowed[None, None], scores, -jnp.inf)
        highest = jnp.max(scores, axis=-1, keepdims=True)
        weights = jnp.exp(scores - highest)
        probabilities = (weights / jnp.sum(weights, axis=-1, keepdims=True)).astype(jnp.bfloat16)
        probabilities = lax.optimization_barrier(probabilities).astype(jnp.float32)
        mixture = jnp.einsum("kgtj,jkd->tkgd", probabilities, value_row_matrix)
        attended = mixture.astype(jnp.bfloat16).reshape(BLOCK_TOKENS, QUERY_HEADS * HEAD_SIZE)
        return jnp.dot(attended, w_reward, preferred_element_type=jnp.float32)

    reward = lax.map(attend_beam, (queries, new_kv, parent_kv, ancestors, ancestor_count))
    kept_blocks = jnp.take(new_kv, keep_list, axis=0)
    return reward, kept_blocks
```

```python
import functools

import jax
import jax.numpy as jnp
from jax import lax
from jax.experimental import pallas as pl
from jax.experimental.pallas import tpu as pltpu
from jax.sharding import PartitionSpec as P

F32 = jnp.float32
BF = jnp.bfloat16
HEAD = 128
NBEAM = 32
NZ = 8
BEAMS = 16
GROUPS = 8
POOL = 12
ANC = 5
HEADS = 8
SCALE2 = HEAD**-0.5 * 1.4426950408889634
NEG = -1e30
NT = (((1,), (1,)), ((), ()))
TN = (((0,), (0,)), ((), ()))
MESH = pl.DeviceIdType.MESH


def head_select(rows):
    r = lax.broadcasted_iota(jnp.int32, (rows, HEADS * HEAD), 0)
    h = lax.broadcasted_iota(jnp.int32, (rows, HEADS * HEAD), 1) // HEAD
    return jnp.where(r % HEADS == h, 1.0, 0.0).astype(BF)


def fold8(x):
    return jnp.sum(x.reshape(16, 8, HEAD), axis=0)


def value_terms(w16, anc, own, vwb, wrep):
    wrep[...] = lax.dot_general(w16, head_select(16), TN, preferred_element_type=F32).astype(BF)

    def pool(i, carry):
        r = jnp.dot(anc[i, 1], wrep[...], preferred_element_type=F32)
        for h in range(HEADS):
            vwb[i, h] = r[:, h * HEAD : (h + 1) * HEAD]
        return carry

    def new(i, carry):
        r = jnp.dot(own[i, 1], wrep[...], preferred_element_type=F32)
        for h in range(HEADS):
            vwb[POOL + i, h] = r[:, h * HEAD : (h + 1) * HEAD]
        return carry

    lax.fori_loop(0, POOL, pool, 0)
    lax.fori_loop(0, BEAMS, new, 0)


def two_heads(q, b, hp):
    lo = hp * 2 * HEAD
    return jnp.concatenate([q[b, :, lo : lo + HEAD], q[b, :, lo + HEAD : lo + 2 * HEAD]], axis=0)


def attend_local(slot_block, slot_live, q, anc, own, vwb, kb, s0, s1, m0, m1, stm, stn, std, lo, hi):
    row = lax.broadcasted_iota(jnp.int32, (HEAD, 2 * HEAD), 0)
    col = lax.broadcasted_iota(jnp.int32, (HEAD, 2 * HEAD), 1) % HEAD
    causal = row <= col
    own_at = ANC * HEAD

    def gather(b):
        for a in range(ANC):
            kb[a * HEAD : (a + 1) * HEAD, :] = anc[slot_block(b, a), 0]
        kb[own_at : own_at + HEAD, :] = own[b, 0]

    def scores(b, hp, s, m):
        r = lax.dot_general(kb[...], two_heads(q, b, hp), NT, preferred_element_type=F32)
        ra = r[:own_at]
        ro = jnp.where(causal, r[own_at:], NEG)
        s[0:own_at, :] = ra
        s[own_at : own_at + HEAD, :] = ro
        mm = jnp.maximum(jnp.max(ra, axis=0, keepdims=True), jnp.max(ro, axis=0, keepdims=True))
        m[0:1, :] = mm * SCALE2

    def weigh(b, hp, s, m):
        for j in range(2):
            h = 2 * hp + j
            mj = m[0:1, j * HEAD : (j + 1) * HEAD]
            num = jnp.zeros((8, HEAD), F32)
            den = jnp.zeros((8, HEAD), F32)
            for a in range(ANC + 1):
                v = slot_block(b, a) if a < ANC else POOL + b
                e = jnp.exp2(s[a * HEAD : (a + 1) * HEAD, j * HEAD : (j + 1) * HEAD] * SCALE2 - mj)
                d_part = fold8(e)
                n_part = fold8(e * vwb[v, h])
                if 0 < a < ANC:
                    live = slot_live(b, a)
                    d_part = d_part * live
                    n_part = n_part * live
                num = num + n_part
                den = den + d_part
            stm[b, h : h + 1, :] = mj
            stn[b, h : h + 1, :] = jnp.sum(num, axis=0, keepdims=True)
            std[b, h : h + 1, :] = jnp.sum(den, axis=0, keepdims=True)

    gather(lo)
    scores(lo, 0, s0, m0)

    def body(b, carry):
        later = jnp.minimum(b + 1, hi - 1)
        scores(b, 1, s1, m1)
        weigh(b, 0, s0, m0)
        scores(b, 2, s0, m0)
        weigh(b, 1, s1, m1)
        scores(b, 3, s1, m1)
        weigh(b, 2, s0, m0)
        gather(later)
        scores(later, 0, s0, m0)
        weigh(b, 3, s1, m1)
        return carry

    lax.fori_loop(lo, hi, body, 0)


def attend_parent(q, pbuf, vwp, stm, stn, std, rew):
    pick = head_select(16)

    def group(g, carry):
        r = lax.dot_general(pbuf[g, HEAD : HEAD + 16, :], pick, TN, preferred_element_type=F32)
        for h in range(HEADS):
            vwp[h] = r[:, h * HEAD : (h + 1) * HEAD]
        for c in range(2):
            b = 2 * g + c
            acc = jnp.zeros((1, HEAD), F32)
            for hp in range(4):
                s = lax.dot_general(pbuf[g, 0:HEAD, :], two_heads(q, b, hp), NT, preferred_element_type=F32)
                for j in range(2):
                    h = 2 * hp + j
                    sj = s[:, j * HEAD : (j + 1) * HEAD]
                    mb = jnp.max(sj, axis=0, keepdims=True) * SCALE2
                    ma = stm[b, h : h + 1, :]
                    m = jnp.maximum(ma, mb)
                    e = jnp.exp2(sj * SCALE2 - m)
                    f = jnp.exp2(ma - m)
                    den = jnp.sum(fold8(e), axis=0, keepdims=True) + std[b, h : h + 1, :] * f
                    num = jnp.sum(fold8(e * vwp[h]), axis=0, keepdims=True) + stn[b, h : h + 1, :] * f
                    acc = acc + num / den
            rew[pl.ds(b, 1), :] = acc
        return carry

    lax.fori_loop(0, GROUPS, group, 0)


def parent_helper(u):
    y = u // 2
    chip = jnp.where(u < 8, 4 * y + y % 2 + 2 * (u % 2), 6)
    return 2 * chip + 1 - (chip // 4) % 2


def keep_helper(t):
    return 2 * t + (t // 4) % 2


def kernel(
    parent, keep, ancestors, count, w, q_hbm, new_hbm, newest_hbm, anc_hbm,
    rew_out, kept_out,
    q, own, newv, anc, vwt, mid, pack, pbuf, zbuf, rew,
    vwb, wrep, kb, s0, s1, m0, m1, stm, stn, std, vwp,
    load_sem, p1_send, p1_recv, p2_send, par_recv, keep_recv, z_send, z_recv,
):
    me = lax.axis_index("beam")
    z = lax.axis_index("mp")
    chip = me // 2
    core = me % 2
    chip_y = chip // 4
    chip_x = chip % 4
    keeps = core == chip_y % 2
    tile_even = (chip_x + chip_y) % 2 == 0
    parents = jnp.logical_and(core != chip_y % 2, jnp.logical_or(tile_even, chip == 6))
    tile_u = jnp.where(tile_even, 2 * chip_y + (chip_x - chip_y % 2) // 2, 8)

    barrier = pltpu.get_barrier_semaphore()

    def greet(o, carry):
        pl.semaphore_signal(barrier, inc=1, device_id=(lax.rem(me + o, NBEAM), z), device_id_type=MESH)
        return carry

    def greet_z(o, carry):
        pl.semaphore_signal(barrier, inc=1, device_id=(me, lax.rem(z + o, NZ)), device_id_type=MESH)
        return carry

    lax.fori_loop(1, NBEAM, greet, 0)
    lax.fori_loop(1, NZ, greet_z, 0)
    loads = [
        pltpu.make_async_copy(newest_hbm.at[:, 1], newv, load_sem.at[0]),
        pltpu.make_async_copy(anc_hbm, anc, load_sem.at[1]),
        pltpu.make_async_copy(new_hbm, own, load_sem.at[2]),
        pltpu.make_async_copy(q_hbm, q, load_sem.at[3]),
    ]
    for load in loads:
        load.start()
    pl.semaphore_wait(barrier, NBEAM - 1 + NZ - 1)

    mine = pl.ds(me * BEAMS, BEAMS)

    def spread(src, peer):
        @pl.when(peer != me)
        def _():
            pltpu.make_async_remote_copy(
                src_ref=src, dst_ref=mid.at[mine], send_sem=p1_send, recv_sem=p1_recv,
                device_id=(peer, z), device_id_type=MESH,
            ).start()

        @pl.when(peer == me)
        def _():
            pltpu.make_async_copy(src, mid.at[mine], p1_recv).start()

    def spread_parent(o, carry):
        u = lax.rem(me + o, 8)
        spread(newest_hbm.at[:, 0, pl.ds(u * 16, 16), :], parent_helper(u))
        return carry

    lax.fori_loop(0, 8, spread_parent, 0)

    w16 = jnp.concatenate([w[...].astype(F32), jnp.zeros((8, HEAD), F32)], axis=0).astype(BF)
    loads[0].wait()

    def value_tile(i, carry):
        r = lax.dot_general(w16, newv[i], NT, preferred_element_type=F32)[:8]
        top = r.astype(BF).astype(F32)
        vwt[i] = jnp.concatenate([top, r - top], axis=0).astype(BF)
        return carry

    lax.fori_loop(0, BEAMS, value_tile, 0)
    spread(vwt, parent_helper(8))

    def spread_keep(o, carry):
        t = lax.rem(chip + o, 16)
        kv = t // 8
        spread(new_hbm.at[:, kv, pl.ds((t % 8) * 16, 16), :], keep_helper(t))
        return carry

    lax.fori_loop(0, 16, spread_keep, 0)

    def hand_on(index, dst, recv):
        pltpu.make_async_copy(mid, mid, p1_recv).wait()

        def to(o, carry):
            d = lax.rem(me + o, NBEAM)
            for k in range(GROUPS):
                pack[d, k] = mid[index(d, k)]

            @pl.when(d != me)
            def _():
                pltpu.make_async_remote_copy(
                    src_ref=pack.at[d], dst_ref=dst, send_sem=p2_send, recv_sem=recv,
                    device_id=(d, z), device_id_type=MESH,
                ).start()

            @pl.when(d == me)
            def _():
                pltpu.make_async_copy(pack.at[d], dst, recv).start()

            return carry

        lax.fori_loop(0, NBEAM, to, 0)

    loads[1].wait()
    loads[2].wait()
    value_terms(w16, anc, own, vwb, wrep)

    @pl.when(parents)
    def _():
        rows = pl.ds(tile_u * 16, 16)
        hand_on(lambda d, k: parent[d * BEAMS + 2 * k], pbuf.at[:, rows, :], par_recv)

    loads[3].wait()

    def slot_block(b, a):
        return lax.rem(jnp.where(a < count[b], ancestors[b, a], ancestors[b, 0]), POOL)

    def slot_live(b, a):
        return jnp.where(a < count[b], 1.0, 0.0)

    local = functools.partial(
        attend_local, slot_block, slot_live, q, anc, own, vwb, kb, s0, s1, m0, m1, stm, stn, std
    )
    local(0, 8)

    @pl.when(keeps)
    def _():
        rows = pl.ds(chip * 16, 16)
        hand_on(lambda d, k: keep[d * GROUPS + k], kept_out.at[:, rows, :], keep_recv)

    local(8, 16)
    pltpu.make_async_copy(pbuf, pbuf, par_recv).wait()
    attend_parent(q, pbuf, vwp, stm, stn, std, rew)

    zbuf[z] = rew[...]

    def send_z(o, carry):
        pltpu.make_async_remote_copy(
            src_ref=rew, dst_ref=zbuf.at[z], send_sem=z_send, recv_sem=z_recv,
            device_id=(me, lax.rem(z + o, NZ)), device_id_type=MESH,
        ).start()
        return carry

    lax.fori_loop(1, NZ, send_z, 0)
    part = zbuf.at[pl.ds(0, NZ - 1)]
    pltpu.make_async_copy(part, part, z_recv).wait()
    total = zbuf[0]
    for i in range(1, NZ):
        total = total + zbuf[i]
    rew_out[...] = total
    pltpu.make_async_copy(part, part, z_send).wait()
    pltpu.make_async_copy(kept_out, kept_out, keep_recv).wait()

    helper = jnp.logical_or(keeps, parents)

    @pl.when(helper)
    def _():
        sent = mid.at[pl.ds(0, 24 * BEAMS)]
        pltpu.make_async_copy(sent, sent, p1_send).wait()
        passed = pack.at[pl.ds(0, NBEAM - 1)]
        pltpu.make_async_copy(passed, passed, p2_send).wait()

    @pl.when(jnp.logical_not(helper))
    def _():
        sent = mid.at[pl.ds(0, 25 * BEAMS)]
        pltpu.make_async_copy(sent, sent, p1_send).wait()


def on_device(
    queries, new_kv, newest_key_value, ancestor_block_store, parent, ancestors, ancestor_count, keep_list, w_reward
):
    smem = pl.BlockSpec(memory_space=pltpu.SMEM)
    vmem = pl.BlockSpec(memory_space=pltpu.VMEM)
    hbm = pl.BlockSpec(memory_space=pl.ANY)
    dma = pltpu.SemaphoreType.DMA
    reward, kept = pl.pallas_call(
        kernel,
        out_shape=(
            jax.ShapeDtypeStruct((BEAMS, HEAD), F32),
            jax.ShapeDtypeStruct((GROUPS, 2 * HEAD, HEAD), BF),
        ),
        in_specs=[smem, smem, smem, smem, vmem, hbm, hbm, hbm, hbm],
        out_specs=(vmem, hbm),
        scratch_shapes=[
            pltpu.VMEM((BEAMS, HEAD, HEADS * HEAD), BF),
            pltpu.VMEM((BEAMS, 2, HEAD, HEAD), BF),
            pltpu.VMEM((BEAMS, HEAD, HEAD), BF),
            pltpu.VMEM((POOL, 2, HEAD, HEAD), BF),
            pltpu.VMEM((BEAMS, 16, HEAD), BF),
            pltpu.VMEM((NBEAM * BEAMS, 16, HEAD), BF),
            pltpu.VMEM((NBEAM, GROUPS, 16, HEAD), BF),
            pltpu.VMEM((GROUPS, HEAD + 16, HEAD), BF),
            pltpu.VMEM((NZ, BEAMS, HEAD), F32),
            pltpu.VMEM((BEAMS, HEAD), F32),
            pltpu.VMEM((POOL + BEAMS, HEADS, HEAD, HEAD), F32),
            pltpu.VMEM((HEAD, HEADS * HEAD), BF),
            pltpu.VMEM((6 * HEAD, HEAD), BF),
            pltpu.VMEM((6 * HEAD, 2 * HEAD), F32),
            pltpu.VMEM((6 * HEAD, 2 * HEAD), F32),
            pltpu.VMEM((8, 2 * HEAD), F32),
            pltpu.VMEM((8, 2 * HEAD), F32),
            pltpu.VMEM((BEAMS, HEADS, HEAD), F32),
            pltpu.VMEM((BEAMS, HEADS, HEAD), F32),
            pltpu.VMEM((BEAMS, HEADS, HEAD), F32),
            pltpu.VMEM((HEADS, HEAD, HEAD), F32),
            dma((4,)), dma, dma, dma, dma, dma, dma, dma,
        ],
        compiler_params=pltpu.CompilerParams(
            collective_id=0, has_side_effects=True, vmem_limit_bytes=56 << 20
        ),
        name="tree_step",
    )(
        parent, keep_list, ancestors, ancestor_count, w_reward.reshape(HEADS, HEAD),
        queries, new_kv, newest_key_value, ancestor_block_store,
    )
    return reward, kept.reshape(GROUPS, 2, HEAD, HEAD)


def solution(mesh):
    placed = (
        P("beam", None, "mp"),
        P("beam", None, None, "mp"),
        P("beam", None, None, "mp"),
        P("beam", None, None, "mp"),
        P(),
        P("beam", None),
        P("beam"),
        P(),
        P("mp"),
    )
    return jax.shard_map(
        on_device,
        mesh=mesh,
        in_specs=placed,
        out_specs=(P("beam", None), P("beam", None, None, "mp")),
        check_vma=False,
    )
```

```python
import functools

import jax
import jax.numpy as jnp
from jax import lax
from jax.experimental import pallas as pl
from jax.experimental.pallas import tpu as pltpu
from jax.sharding import PartitionSpec as P

F32 = jnp.float32
BF = jnp.bfloat16
HEAD = 128
NBEAM = 32
BEAMS = 16
GROUPS = 8
POOL = 12
ANC = 5
HEADS = 8
SCALE2 = HEAD**-0.5 * 1.4426950408889634
NEG = -1e30
NT = (((1,), (1,)), ((), ()))
TN = (((0,), (0,)), ((), ()))
MESH = pl.DeviceIdType.MESH


def head_select(rows):
    r = lax.broadcasted_iota(jnp.int32, (rows, HEADS * HEAD), 0)
    h = lax.broadcasted_iota(jnp.int32, (rows, HEADS * HEAD), 1) // HEAD
    return jnp.where(r % HEADS == h, 1.0, 0.0).astype(BF)


def fold8(x):
    return jnp.sum(x.reshape(16, 8, HEAD), axis=0)


def value_terms(w16, anc, own, vwb, wrep):
    wrep[...] = lax.dot_general(w16, head_select(16), TN, preferred_element_type=F32).astype(BF)

    def put(block, at):
        r = jnp.dot(block, wrep[...], preferred_element_type=F32)
        for h in range(HEADS):
            vwb[at, h] = r[:, h * HEAD : (h + 1) * HEAD]

    def pool(i, carry):
        for u in range(4):
            put(anc[4 * i + u, 1], 4 * i + u)
        return carry

    def new(i, carry):
        for u in range(4):
            put(own[4 * i + u, 1], POOL + 4 * i + u)
        return carry

    lax.fori_loop(0, POOL // 4, pool, 0)
    lax.fori_loop(0, BEAMS // 4, new, 0)


def two_heads(q, b, hp):
    lo = hp * 2 * HEAD
    return jnp.concatenate([q[b, :, lo : lo + HEAD], q[b, :, lo + HEAD : lo + 2 * HEAD]], axis=0)


def attend_local(slot_block, slot_live, q, anc, own, vwb, kb, s0, s1, m0, m1, stm, stn, std, lo, hi):
    row = lax.broadcasted_iota(jnp.int32, (HEAD, 2 * HEAD), 0)
    col = lax.broadcasted_iota(jnp.int32, (HEAD, 2 * HEAD), 1) % HEAD
    causal = row <= col
    own_at = ANC * HEAD

    def gather(b):
        for a in range(ANC):
            kb[a * HEAD : (a + 1) * HEAD, :] = anc[slot_block(b, a), 0]
        kb[own_at : own_at + HEAD, :] = own[b, 0]

    def scores(b, hp, s, m):
        r = lax.dot_general(kb[...], two_heads(q, b, hp), NT, preferred_element_type=F32)
        ra = r[:own_at]
        ro = jnp.where(causal, r[own_at:], NEG)
        s[0:own_at, :] = ra
        s[own_at : own_at + HEAD, :] = ro
        mm = jnp.maximum(jnp.max(ra, axis=0, keepdims=True), jnp.max(ro, axis=0, keepdims=True))
        m[0:1, :] = mm * SCALE2

    def weigh(b, hp, s, m):
        for j in range(2):
            h = 2 * hp + j
            mj = m[0:1, j * HEAD : (j + 1) * HEAD]
            num = jnp.zeros((8, HEAD), F32)
            den = jnp.zeros((8, HEAD), F32)
            for a in range(ANC + 1):
                v = slot_block(b, a) if a < ANC else POOL + b
                e = jnp.exp2(s[a * HEAD : (a + 1) * HEAD, j * HEAD : (j + 1) * HEAD] * SCALE2 - mj)
                d_part = fold8(e)
                n_part = fold8(e * vwb[v, h])
                if 0 < a < ANC:
                    live = slot_live(b, a)
                    d_part = d_part * live
                    n_part = n_part * live
                num = num + n_part
                den = den + d_part
            stm[b, h : h + 1, :] = mj
            stn[b, h : h + 1, :] = jnp.sum(num, axis=0, keepdims=True)
            std[b, h : h + 1, :] = jnp.sum(den, axis=0, keepdims=True)

    gather(lo)
    scores(lo, 0, s0, m0)

    def body(b, carry):
        later = jnp.minimum(b + 1, hi - 1)
        scores(b, 1, s1, m1)
        weigh(b, 0, s0, m0)
        scores(b, 2, s0, m0)
        weigh(b, 1, s1, m1)
        scores(b, 3, s1, m1)
        weigh(b, 2, s0, m0)
        gather(later)
        scores(later, 0, s0, m0)
        weigh(b, 3, s1, m1)
        return carry

    lax.fori_loop(lo, hi, body, 0)


def attend_parent(q, pbuf, stm, stn, std, rew):
    pick = head_select(16)

    def beam(g, b, terms):
        scores, tops = [], []
        for hp in range(4):
            s = lax.dot_general(pbuf[g, 0:HEAD, :], two_heads(q, b, hp), NT, preferred_element_type=F32)
            top = jnp.max(s, axis=0, keepdims=True)
            for j in range(2):
                scores.append(s[:, j * HEAD : (j + 1) * HEAD])
                tops.append(top[:, j * HEAD : (j + 1) * HEAD])
        ma = stm[b]
        m = jnp.maximum(ma, jnp.concatenate(tops, axis=0) * SCALE2)
        f = jnp.exp2(ma - m)
        dens, nums = [], []
        for h in range(HEADS):
            e = jnp.exp2(scores[h] * SCALE2 - m[h : h + 1])
            dens.append(jnp.sum(fold8(e), axis=0, keepdims=True))
            nums.append(jnp.sum(fold8(e * terms[:, h * HEAD : (h + 1) * HEAD]), axis=0, keepdims=True))
        den = jnp.concatenate(dens, axis=0) + std[b] * f
        num = jnp.concatenate(nums, axis=0) + stn[b] * f
        rew[pl.ds(b, 1), :] = jnp.sum(num / den, axis=0, keepdims=True)

    def groups(i, carry):
        for u in range(4):
            g = 4 * i + u
            terms = lax.dot_general(pbuf[g, HEAD : HEAD + 16, :], pick, TN, preferred_element_type=F32)
            for c in range(2):
                beam(g, 2 * g + c, terms)
        return carry

    lax.fori_loop(0, GROUPS // 4, groups, 0)


def parent_helper(u):
    y = u // 2
    chip = jnp.where(u < 8, 4 * y + y % 2 + 2 * (u % 2), 6)
    return 2 * chip + 1 - (chip // 4) % 2


def keep_helper(t):
    return 2 * t + (t // 4) % 2


def ranks(rows):
    wide = [jnp.broadcast_to(r, (HEAD, HEAD)) for r in rows]
    tall = [x.T for x in wide]
    earlier = lax.broadcasted_iota(jnp.int32, (HEAD, HEAD), 0) < lax.broadcasted_iota(jnp.int32, (HEAD, HEAD), 1)
    out = []
    for j in range(len(rows)):
        same = jnp.where(jnp.logical_and(tall[j] == wide[j], earlier), 1, 0)
        for i in range(j):
            same = same + jnp.where(tall[i] == wide[j], 1, 0)
        out.append(jnp.sum(same, axis=0, keepdims=True))
    return out


def routes(me, x, children):
    rows = [x[c : c + 1, :] for c in range(x.shape[0])]
    source = [lax.shift_right_logical(r, 4) for r in rows]
    place = [lax.shift_right_logical(r, children - 1) for r in ranks(source)]
    index = [jnp.minimum(s * GROUPS + p, NBEAM * GROUPS - 1) for s, p in zip(source, place)]
    slot = lax.broadcasted_iota(jnp.int32, (GROUPS, HEAD), 0)
    lane = lax.broadcasted_iota(jnp.int32, (GROUPS, HEAD), 1)
    first = lax.rem(lane, children) == 0
    given = jnp.zeros((GROUPS, HEAD), jnp.int32)
    for r, s, p in zip(rows, source, place):
        hit = jnp.logical_and(jnp.logical_and(s == me, p == slot), first)
        given = given + jnp.where(hit, lax.rem(r, BEAMS), 0)
    return index, jnp.sum(given, axis=1, keepdims=True)


STEPS = (
    (1, 0), (0, 1), (3, 0), (0, 3), (1, 1), (3, 3), (1, 3), (3, 1),
    (2, 0), (0, 2), (2, 1), (1, 2), (2, 3), (3, 2), (2, 2), (0, 0),
)


def kernel(
    cap,
    parent, keep, ancestors, count, parent_v, keep_v, w, q_hbm, new_hbm, newest_hbm, anc_hbm,
    parts_out, kept_out,
    q, own, newest, anc, given_p, given_k, vwt, mid, pack, pbuf, rew, tab_v, tab,
    vwb, wrep, kb, s0, s1, m0, m1, stm, stn, std,
    load_sem, p1_send, p1_recv, p2_send, par_recv, keep_recv, z_send, z_recv, z_own,
):
    NZ = lax.axis_size("mp")
    me = lax.axis_index("beam")
    z = lax.axis_index("mp")
    chip = me // 2
    core = me % 2
    chip_y = chip // 4
    chip_x = chip % 4
    keeps = core == chip_y % 2
    tile_even = (chip_x + chip_y) % 2 == 0
    parents = jnp.logical_and(core != chip_y % 2, jnp.logical_or(tile_even, chip == 6))
    tile_u = jnp.where(tile_even, 2 * chip_y + (chip_x - chip_y % 2) // 2, 8)

    barrier = pltpu.get_barrier_semaphore()

    def greet(o, carry):
        pl.semaphore_signal(barrier, inc=1, device_id=(lax.rem(me + o, NBEAM), z), device_id_type=MESH)
        return carry

    def greet_z(o, carry):
        pl.semaphore_signal(barrier, inc=1, device_id=(me, lax.rem(z + o, NZ)), device_id_type=MESH)
        return carry

    loads = [
        pltpu.make_async_copy(newest_hbm, newest, load_sem.at[0]),
        pltpu.make_async_copy(new_hbm, own, load_sem.at[1]),
        pltpu.make_async_copy(anc_hbm, anc, load_sem.at[2]),
        pltpu.make_async_copy(q_hbm, q, load_sem.at[3]),
    ]
    lax.fori_loop(1, NBEAM, greet, 0)
    lax.fori_loop(1, NZ, greet_z, 0)
    for load in loads:
        load.start()

    if cap < BEAMS:
        index_p, mine_p = routes(me, parent_v[...], 2)
        index_k, mine_k = routes(me, keep_v[...], 1)
        for c in range(4):
            tab_v[c : c + 1, :] = index_p[c]
        for c in range(2):
            tab_v[4 + c : 5 + c, :] = index_k[c]
        lane = lax.broadcasted_iota(jnp.int32, (GROUPS, HEAD), 1)
        tab_v[8:16, :] = jnp.where(lane == 0, mine_p, mine_k)
        to_smem = pltpu.make_async_copy(tab_v, tab, load_sem.at[4])
        to_smem.start()
        to_smem.wait()
        loads[0].wait()
        for r in range(cap):
            given_p[r] = newest[tab[8 + r, 0], 0]
        tiles_p = given_p

        def value_block(i):
            return newest[tab[8 + i, 0], 1]

        def index_parent(d, k):
            return tab[d // 8, (d % 8) * BEAMS + 2 * k]

        def index_keep(d, k):
            return tab[4 + d // 16, (d % 16) * GROUPS + k]

    else:
        loads[0].wait()
        tiles_p = newest.at[:, 0]

        def value_block(i):
            return newest[i, 1]

        def index_parent(d, k):
            return parent[d * BEAMS + 2 * k]

        def index_keep(d, k):
            return keep[d * GROUPS + k]

    pl.semaphore_wait(barrier, NBEAM - 1 + NZ - 1)

    mine = pl.ds(me * cap, cap)

    def spread(src, peer):
        @pl.when(peer != me)
        def _():
            pltpu.make_async_remote_copy(
                src_ref=src, dst_ref=mid.at[mine], send_sem=p1_send, recv_sem=p1_recv,
                device_id=(peer, z), device_id_type=MESH,
            ).start()

        @pl.when(peer == me)
        def _():
            pltpu.make_async_copy(src, mid.at[mine], p1_recv).start()

    def spread_parent(o, carry):
        u = lax.rem(me + o, 8)
        spread(tiles_p.at[:, pl.ds(u * 16, 16), :], parent_helper(u))
        return carry

    lax.fori_loop(0, 8, spread_parent, 0)

    w16 = jnp.concatenate([w[...].astype(F32), jnp.zeros((8, HEAD), F32)], axis=0).astype(BF)

    def value_tile(i, carry):
        for u in range(4):
            r = lax.dot_general(w16, value_block(4 * i + u), NT, preferred_element_type=F32)[:8]
            top = r.astype(BF).astype(F32)
            vwt[4 * i + u] = jnp.concatenate([top, r - top], axis=0).astype(BF)
        return carry

    lax.fori_loop(0, cap // 4, value_tile, 0)
    spread(vwt, parent_helper(8))

    loads[1].wait()
    if cap < BEAMS:
        for r in range(cap):
            given_k[r] = own[tab[8 + r, 1]]
        tiles_k = given_k
    else:
        tiles_k = own

    for dx, dy in STEPS:
        t = ((chip_y + dy) % 4) * 4 + (chip_x + dx) % 4
        spread(tiles_k.at[:, t // 8, pl.ds((t % 8) * 16, 16), :], keep_helper(t))

    def hand_on(index, dst, recv):
        pltpu.make_async_copy(mid, mid, p1_recv).wait()

        def to(o, carry):
            d = lax.rem(me + o, NBEAM)
            for k in range(GROUPS):
                pack[d, k] = mid[index(d, k)]

            @pl.when(d != me)
            def _():
                pltpu.make_async_remote_copy(
                    src_ref=pack.at[d], dst_ref=dst, send_sem=p2_send, recv_sem=recv,
                    device_id=(d, z), device_id_type=MESH,
                ).start()

            @pl.when(d == me)
            def _():
                pltpu.make_async_copy(pack.at[d], dst, recv).start()

            return carry

        lax.fori_loop(0, NBEAM, to, 0)

    loads[2].wait()
    value_terms(w16, anc, own, vwb, wrep)

    @pl.when(parents)
    def _():
        rows = pl.ds(tile_u * 16, 16)
        hand_on(index_parent, pbuf.at[:, rows, :], par_recv)

    loads[3].wait()

    def slot_block(b, a):
        return lax.rem(jnp.where(a < count[b], ancestors[a, b], ancestors[0, b]), POOL)

    def slot_live(b, a):
        return jnp.where(a < count[b], 1.0, 0.0)

    local = functools.partial(
        attend_local, slot_block, slot_live, q, anc, own, vwb, kb, s0, s1, m0, m1, stm, stn, std
    )
    local(0, FIRST)

    @pl.when(keeps)
    def _():
        rows = pl.ds(chip * 16, 16)
        hand_on(index_keep, kept_out.at[:, rows, :], keep_recv)

    local(FIRST, BEAMS)
    pltpu.make_async_copy(pbuf, pbuf, par_recv).wait()
    attend_parent(q, pbuf, stm, stn, std, rew)

    own_part = pltpu.make_async_copy(rew, parts_out.at[z], z_own)
    own_part.start()

    def send_z(o, carry):
        pltpu.make_async_remote_copy(
            src_ref=rew, dst_ref=parts_out.at[z], send_sem=z_send, recv_sem=z_recv,
            device_id=(me, lax.rem(z + o, NZ)), device_id_type=MESH,
        ).start()
        return carry

    lax.fori_loop(1, NZ, send_z, 0)
    own_part.wait()
    part = parts_out.at[pl.ds(0, NZ - 1)]
    pltpu.make_async_copy(part, part, z_recv).wait()
    pltpu.make_async_copy(part, part, z_send).wait()
    pltpu.make_async_copy(kept_out, kept_out, keep_recv).wait()

    helper = jnp.logical_or(keeps, parents)

    @pl.when(helper)
    def _():
        sent = mid.at[pl.ds(0, 24 * cap)]
        pltpu.make_async_copy(sent, sent, p1_send).wait()
        passed = pack.at[pl.ds(0, NBEAM - 1)]
        pltpu.make_async_copy(passed, passed, p2_send).wait()

    @pl.when(jnp.logical_not(helper))
    def _():
        sent = mid.at[pl.ds(0, 25 * cap)]
        pltpu.make_async_copy(sent, sent, p1_send).wait()


FIRST = 6
SMEM = pl.BlockSpec(memory_space=pltpu.SMEM)
VMEM = pl.BlockSpec(memory_space=pltpu.VMEM)
HBM = pl.BlockSpec(memory_space=pl.ANY)


def tree_step(cap, *operands):
    NZ = lax.axis_size("mp")
    dma = pltpu.SemaphoreType.DMA
    return pl.pallas_call(
        functools.partial(kernel, cap),
        out_shape=(
            jax.ShapeDtypeStruct((NZ, BEAMS, HEAD), F32),
            jax.ShapeDtypeStruct((GROUPS, 2 * HEAD, HEAD), BF),
        ),
        in_specs=[SMEM, SMEM, SMEM, SMEM, VMEM, VMEM, VMEM, HBM, HBM, HBM, HBM],
        out_specs=(HBM, HBM),
        scratch_shapes=[
            pltpu.VMEM((BEAMS, HEAD, HEADS * HEAD), BF),
            pltpu.VMEM((BEAMS, 2, HEAD, HEAD), BF),
            pltpu.VMEM((BEAMS, 2, HEAD, HEAD), BF),
            pltpu.VMEM((POOL, 2, HEAD, HEAD), BF),
            pltpu.VMEM((GROUPS, HEAD, HEAD), BF),
            pltpu.VMEM((GROUPS, 2, HEAD, HEAD), BF),
            pltpu.VMEM((cap, 16, HEAD), BF),
            pltpu.VMEM((NBEAM * cap, 16, HEAD), BF),
            pltpu.VMEM((NBEAM, GROUPS, 16, HEAD), BF),
            pltpu.VMEM((GROUPS, HEAD + 16, HEAD), BF),
            pltpu.VMEM((BEAMS, HEAD), F32),
            pltpu.VMEM((16, HEAD), jnp.int32),
            pltpu.SMEM((16, HEAD), jnp.int32),
            pltpu.VMEM((POOL + BEAMS, HEADS, HEAD, HEAD), F32),
            pltpu.VMEM((HEAD, HEADS * HEAD), BF),
            pltpu.VMEM((6 * HEAD, HEAD), BF),
            pltpu.VMEM((6 * HEAD, 2 * HEAD), F32),
            pltpu.VMEM((6 * HEAD, 2 * HEAD), F32),
            pltpu.VMEM((8, 2 * HEAD), F32),
            pltpu.VMEM((8, 2 * HEAD), F32),
            pltpu.VMEM((BEAMS, HEADS, HEAD), F32),
            pltpu.VMEM((BEAMS, HEADS, HEAD), F32),
            pltpu.VMEM((BEAMS, HEADS, HEAD), F32),
            dma((5,)), dma, dma, dma, dma, dma, dma, dma, dma,
        ],
        compiler_params=pltpu.CompilerParams(
            collective_id=cap, has_side_effects=True, vmem_limit_bytes=56 << 20
        ),
        name="tree_step_%d" % cap,
    )(*operands)


def finish_kernel(parts, kept_in, rew_out, kept_out, sem):
    copy = pltpu.make_async_copy(kept_in, kept_out, sem)
    copy.start()
    total = parts[0]
    for i in range(1, parts.shape[0]):
        total = total + parts[i]
    rew_out[...] = total
    copy.wait()


def on_device(
    queries, new_kv, newest_key_value, ancestor_block_store, parent, ancestors, ancestor_count, keep_list, w_reward
):
    device = jnp.arange(NBEAM, dtype=jnp.int32)
    gives_p = jnp.sum((parent[:, None] // BEAMS == device).astype(jnp.int32), axis=0)
    gives_k = jnp.sum((keep_list[:, None] // BEAMS == device).astype(jnp.int32), axis=0)
    even = jnp.max(jnp.maximum(gives_p, 2 * gives_k)) <= 2 * GROUPS
    parts, kept = lax.cond(
        even,
        functools.partial(tree_step, GROUPS),
        functools.partial(tree_step, BEAMS),
        parent, keep_list, ancestors.T, ancestor_count, parent.reshape(4, HEAD), keep_list.reshape(2, HEAD),
        w_reward.reshape(HEADS, HEAD), queries, new_kv, newest_key_value, ancestor_block_store,
    )
    reward, kept = pl.pallas_call(
        finish_kernel,
        out_shape=(
            jax.ShapeDtypeStruct((BEAMS, HEAD), F32),
            jax.ShapeDtypeStruct((GROUPS, 2 * HEAD, HEAD), BF),
        ),
        in_specs=[VMEM, HBM],
        out_specs=(VMEM, HBM),
        scratch_shapes=[pltpu.SemaphoreType.DMA],
        name="finish",
    )(parts, kept)
    return reward, kept.reshape(GROUPS, 2, HEAD, HEAD)


def solution(mesh):
    placed = (
        P("beam", None, "mp"),
        P("beam", None, None, "mp"),
        P("beam", None, None, "mp"),
        P("beam", None, None, "mp"),
        P(),
        P("beam", None),
        P("beam"),
        P(),
        P("mp"),
    )
    return jax.shard_map(
        on_device,
        mesh=mesh,
        in_specs=placed,
        out_specs=(P("beam", None), P("beam", None, None, "mp")),
        check_vma=False,
    )
```

```python
import functools

import jax
import jax.numpy as jnp
from jax import lax
from jax.experimental import pallas as pl
from jax.experimental.pallas import tpu as pltpu
from jax.sharding import PartitionSpec as P

F32 = jnp.float32
BF = jnp.bfloat16
HEAD = 128
NBEAM = 32
BEAMS = 16
GROUPS = 8
POOL = 12
ANC = 5
HEADS = 8
SCALE2 = HEAD**-0.5 * 1.4426950408889634
NEG = -1e30
NT = (((1,), (1,)), ((), ()))
TN = (((0,), (0,)), ((), ()))
MESH = pl.DeviceIdType.MESH


def head_select(rows):
    r = lax.broadcasted_iota(jnp.int32, (rows, HEADS * HEAD), 0)
    h = lax.broadcasted_iota(jnp.int32, (rows, HEADS * HEAD), 1) // HEAD
    return jnp.where(r % HEADS == h, 1.0, 0.0).astype(BF)


def fold8(x):
    return jnp.sum(x.reshape(16, 8, HEAD), axis=0)


def value_terms(w16, anc, own, vwb, wrep):
    wrep[...] = lax.dot_general(w16, head_select(16), TN, preferred_element_type=F32).astype(BF)

    def put(block, at):
        r = jnp.dot(block, wrep[...], preferred_element_type=F32)
        for h in range(HEADS):
            vwb[at, h] = r[:, h * HEAD : (h + 1) * HEAD]

    def pool(i, carry):
        for u in range(4):
            put(anc[4 * i + u, 1], 4 * i + u)
        return carry

    def new(i, carry):
        for u in range(4):
            put(own[4 * i + u, 1], POOL + 4 * i + u)
        return carry

    lax.fori_loop(0, POOL // 4, pool, 0)
    lax.fori_loop(0, BEAMS // 4, new, 0)


def two_heads(q, b, hp):
    lo = hp * 2 * HEAD
    return jnp.concatenate([q[b, :, lo : lo + HEAD], q[b, :, lo + HEAD : lo + 2 * HEAD]], axis=0)


def attend_local(slot_block, slot_live, q, anc, own, vwb, kb, s0, s1, m0, m1, stm, stn, std, lo, hi):
    row = lax.broadcasted_iota(jnp.int32, (HEAD, 2 * HEAD), 0)
    col = lax.broadcasted_iota(jnp.int32, (HEAD, 2 * HEAD), 1) % HEAD
    causal = row <= col
    own_at = ANC * HEAD

    def gather(b):
        for a in range(ANC):
            kb[a * HEAD : (a + 1) * HEAD, :] = anc[slot_block(b, a), 0]
        kb[own_at : own_at + HEAD, :] = own[b, 0]

    def scores(b, hp, s, m):
        r = lax.dot_general(kb[...], two_heads(q, b, hp), NT, preferred_element_type=F32)
        ra = r[:own_at]
        ro = jnp.where(causal, r[own_at:], NEG)
        s[0:own_at, :] = ra
        s[own_at : own_at + HEAD, :] = ro
        mm = jnp.maximum(jnp.max(ra, axis=0, keepdims=True), jnp.max(ro, axis=0, keepdims=True))
        m[0:1, :] = mm * SCALE2

    def weigh(b, hp, s, m):
        for j in range(2):
            h = 2 * hp + j
            mj = m[0:1, j * HEAD : (j + 1) * HEAD]
            num = jnp.zeros((8, HEAD), F32)
            den = jnp.zeros((8, HEAD), F32)
            for a in range(ANC + 1):
                v = slot_block(b, a) if a < ANC else POOL + b
                e = jnp.exp2(s[a * HEAD : (a + 1) * HEAD, j * HEAD : (j + 1) * HEAD] * SCALE2 - mj)
                d_part = fold8(e)
                n_part = fold8(e * vwb[v, h])
                if 0 < a < ANC:
                    live = slot_live(b, a)
                    d_part = d_part * live
                    n_part = n_part * live
                num = num + n_part
                den = den + d_part
            stm[b, h : h + 1, :] = mj
            stn[b, h : h + 1, :] = jnp.sum(num, axis=0, keepdims=True)
            std[b, h : h + 1, :] = jnp.sum(den, axis=0, keepdims=True)

    gather(lo)
    scores(lo, 0, s0, m0)

    def body(b, carry):
        later = jnp.minimum(b + 1, hi - 1)
        scores(b, 1, s1, m1)
        weigh(b, 0, s0, m0)
        scores(b, 2, s0, m0)
        weigh(b, 1, s1, m1)
        scores(b, 3, s1, m1)
        weigh(b, 2, s0, m0)
        gather(later)
        scores(later, 0, s0, m0)
        weigh(b, 3, s1, m1)
        return carry

    lax.fori_loop(lo, hi, body, 0)


def attend_parent(q, pbuf, stm, stn, std, rew):
    pick = head_select(16)

    def beam(g, b, terms):
        scores, tops = [], []
        for hp in range(4):
            s = lax.dot_general(pbuf[g, 0:HEAD, :], two_heads(q, b, hp), NT, preferred_element_type=F32)
            top = jnp.max(s, axis=0, keepdims=True)
            for j in range(2):
                scores.append(s[:, j * HEAD : (j + 1) * HEAD])
                tops.append(top[:, j * HEAD : (j + 1) * HEAD])
        ma = stm[b]
        m = jnp.maximum(ma, jnp.concatenate(tops, axis=0) * SCALE2)
        f = jnp.exp2(ma - m)
        dens, nums = [], []
        for h in range(HEADS):
            e = jnp.exp2(scores[h] * SCALE2 - m[h : h + 1])
            dens.append(jnp.sum(fold8(e), axis=0, keepdims=True))
            nums.append(jnp.sum(fold8(e * terms[:, h * HEAD : (h + 1) * HEAD]), axis=0, keepdims=True))
        den = jnp.concatenate(dens, axis=0) + std[b] * f
        num = jnp.concatenate(nums, axis=0) + stn[b] * f
        rew[pl.ds(b, 1), :] = jnp.sum(num / den, axis=0, keepdims=True)

    def groups(i, carry):
        for u in range(4):
            g = 4 * i + u
            terms = lax.dot_general(pbuf[g, HEAD : HEAD + 16, :], pick, TN, preferred_element_type=F32)
            for c in range(2):
                beam(g, 2 * g + c, terms)
        return carry

    lax.fori_loop(0, GROUPS // 4, groups, 0)


def parent_helper(u):
    y = u // 2
    chip = jnp.where(u < 8, 4 * y + y % 2 + 2 * (u % 2), 6)
    return 2 * chip + 1 - (chip // 4) % 2


def keep_helper(t):
    return 2 * t + (t // 4) % 2


def ranks(rows):
    wide = [jnp.broadcast_to(r, (HEAD, HEAD)) for r in rows]
    tall = [x.T for x in wide]
    earlier = lax.broadcasted_iota(jnp.int32, (HEAD, HEAD), 0) < lax.broadcasted_iota(jnp.int32, (HEAD, HEAD), 1)
    out = []
    for j in range(len(rows)):
        same = jnp.where(jnp.logical_and(tall[j] == wide[j], earlier), 1, 0)
        for i in range(j):
            same = same + jnp.where(tall[i] == wide[j], 1, 0)
        out.append(jnp.sum(same, axis=0, keepdims=True))
    return out


def routes(me, x, children):
    rows = [x[c : c + 1, :] for c in range(x.shape[0])]
    source = [lax.shift_right_logical(r, 4) for r in rows]
    place = [lax.shift_right_logical(r, children - 1) for r in ranks(source)]
    index = [jnp.minimum(s * GROUPS + p, NBEAM * GROUPS - 1) for s, p in zip(source, place)]
    slot = lax.broadcasted_iota(jnp.int32, (GROUPS, HEAD), 0)
    lane = lax.broadcasted_iota(jnp.int32, (GROUPS, HEAD), 1)
    first = lax.rem(lane, children) == 0
    given = jnp.zeros((GROUPS, HEAD), jnp.int32)
    for r, s, p in zip(rows, source, place):
        hit = jnp.logical_and(jnp.logical_and(s == me, p == slot), first)
        given = given + jnp.where(hit, lax.rem(r, BEAMS), 0)
    return index, jnp.sum(given, axis=1, keepdims=True)


STEPS = (
    (1, 0), (0, 1), (3, 0), (0, 3), (1, 1), (3, 3), (1, 3), (3, 1),
    (2, 0), (0, 2), (2, 1), (1, 2), (2, 3), (3, 2), (2, 2), (0, 0),
)


def kernel(
    cap,
    parent, keep, ancestors, count, parent_v, keep_v, w, q_hbm, new_hbm, newest_hbm, anc_hbm,
    parts_out, kept_out,
    q, own, newest, anc, given_p, given_k, vwt, mid, pack, pbuf, rew, tab_v, tab,
    vwb, wrep, kb, s0, s1, m0, m1, stm, stn, std,
    load_sem, p1_send, p1_recv, p2_send, par_recv, keep_recv, z_send, z_recv, z_own,
):
    NZ = lax.axis_size("mp")
    me = lax.axis_index("beam")
    z = lax.axis_index("mp")
    chip = me // 2
    core = me % 2
    chip_y = chip // 4
    chip_x = chip % 4
    keeps = core == chip_y % 2
    tile_even = (chip_x + chip_y) % 2 == 0
    parents = jnp.logical_and(core != chip_y % 2, jnp.logical_or(tile_even, chip == 6))
    tile_u = jnp.where(tile_even, 2 * chip_y + (chip_x - chip_y % 2) // 2, 8)

    barrier = pltpu.get_barrier_semaphore()

    def greet(o, carry):
        pl.semaphore_signal(barrier, inc=1, device_id=(lax.rem(me + o, NBEAM), z), device_id_type=MESH)
        return carry

    def greet_z(o, carry):
        pl.semaphore_signal(barrier, inc=1, device_id=(me, lax.rem(z + o, NZ)), device_id_type=MESH)
        return carry

    loads = [
        pltpu.make_async_copy(newest_hbm, newest, load_sem.at[0]),
        pltpu.make_async_copy(new_hbm, own, load_sem.at[1]),
        pltpu.make_async_copy(anc_hbm, anc, load_sem.at[2]),
        pltpu.make_async_copy(q_hbm, q, load_sem.at[3]),
    ]
    lax.fori_loop(1, NBEAM, greet, 0)
    lax.fori_loop(1, NZ, greet_z, 0)
    for load in loads:
        load.start()

    if cap < BEAMS:
        index_p, mine_p = routes(me, parent_v[...], 2)
        index_k, mine_k = routes(me, keep_v[...], 1)
        for c in range(4):
            tab_v[c : c + 1, :] = index_p[c]
        for c in range(2):
            tab_v[4 + c : 5 + c, :] = index_k[c]
        lane = lax.broadcasted_iota(jnp.int32, (GROUPS, HEAD), 1)
        tab_v[8:16, :] = jnp.where(lane == 0, mine_p, mine_k)
        to_smem = pltpu.make_async_copy(tab_v, tab, load_sem.at[4])
        to_smem.start()
        to_smem.wait()
        loads[0].wait()
        for r in range(cap):
            given_p[r] = newest[tab[8 + r, 0], 0]
        tiles_p = given_p

        def value_block(i):
            return newest[tab[8 + i, 0], 1]

        def index_parent(d, k):
            return tab[d // 8, (d % 8) * BEAMS + 2 * k]

        def index_keep(d, k):
            return tab[4 + d // 16, (d % 16) * GROUPS + k]

    else:
        loads[0].wait()
        tiles_p = newest.at[:, 0]

        def value_block(i):
            return newest[i, 1]

        def index_parent(d, k):
            return parent[d * BEAMS + 2 * k]

        def index_keep(d, k):
            return keep[d * GROUPS + k]

    pl.semaphore_wait(barrier, NBEAM - 1 + NZ - 1)

    mine = pl.ds(me * cap, cap)

    def spread(src, peer):
        @pl.when(peer != me)
        def _():
            pltpu.make_async_remote_copy(
                src_ref=src, dst_ref=mid.at[mine], send_sem=p1_send, recv_sem=p1_recv,
                device_id=(peer, z), device_id_type=MESH,
            ).start()

        @pl.when(peer == me)
        def _():
            pltpu.make_async_copy(src, mid.at[mine], p1_recv).start()

    def spread_parent(o, carry):
        u = lax.rem(me + o, 8)
        spread(tiles_p.at[:, pl.ds(u * 16, 16), :], parent_helper(u))
        return carry

    lax.fori_loop(0, 8, spread_parent, 0)

    w16 = jnp.concatenate([w[...].astype(F32), jnp.zeros((8, HEAD), F32)], axis=0).astype(BF)

    def value_tile(i, carry):
        for u in range(4):
            r = lax.dot_general(w16, value_block(4 * i + u), NT, preferred_element_type=F32)[:8]
            top = r.astype(BF).astype(F32)
            vwt[4 * i + u] = jnp.concatenate([top, r - top], axis=0).astype(BF)
        return carry

    lax.fori_loop(0, cap // 4, value_tile, 0)
    spread(vwt, parent_helper(8))

    loads[1].wait()
    if cap < BEAMS:
        for r in range(cap):
            given_k[r] = own[tab[8 + r, 1]]
        tiles_k = given_k
    else:
        tiles_k = own

    def spread_keep(steps):
        for dx, dy in steps:
            t = ((chip_y + dy) % 4) * 4 + (chip_x + dx) % 4
            spread(tiles_k.at[:, t // 8, pl.ds((t % 8) * 16, 16), :], keep_helper(t))

    spread_keep(STEPS[:EARLY])

    def hand_on(index, dst, recv):
        pltpu.make_async_copy(mid, mid, p1_recv).wait()

        def to(o, carry):
            d = lax.rem(me + o, NBEAM)
            for k in range(GROUPS):
                pack[d, k] = mid[index(d, k)]

            @pl.when(d != me)
            def _():
                pltpu.make_async_remote_copy(
                    src_ref=pack.at[d], dst_ref=dst, send_sem=p2_send, recv_sem=recv,
                    device_id=(d, z), device_id_type=MESH,
                ).start()

            @pl.when(d == me)
            def _():
                pltpu.make_async_copy(pack.at[d], dst, recv).start()

            return carry

        lax.fori_loop(0, NBEAM, to, 0)

    loads[2].wait()
    value_terms(w16, anc, own, vwb, wrep)

    loads[3].wait()

    def slot_block(b, a):
        return lax.rem(jnp.where(a < count[b], ancestors[a, b], ancestors[0, b]), POOL)

    def slot_live(b, a):
        return jnp.where(a < count[b], 1.0, 0.0)

    local = functools.partial(
        attend_local, slot_block, slot_live, q, anc, own, vwb, kb, s0, s1, m0, m1, stm, stn, std
    )
    spread_keep(STEPS[EARLY:])
    local(0, PARENT_AT)

    @pl.when(parents)
    def _():
        rows = pl.ds(tile_u * 16, 16)
        hand_on(index_parent, pbuf.at[:, rows, :], par_recv)

    local(PARENT_AT, FIRST)

    @pl.when(keeps)
    def _():
        rows = pl.ds(chip * 16, 16)
        hand_on(index_keep, kept_out.at[:, rows, :], keep_recv)

    if FIRST < BEAMS:
        local(FIRST, BEAMS)
    pltpu.make_async_copy(pbuf, pbuf, par_recv).wait()
    attend_parent(q, pbuf, stm, stn, std, rew)

    own_part = pltpu.make_async_copy(rew, parts_out.at[z], z_own)
    own_part.start()

    def send_z(o, carry):
        pltpu.make_async_remote_copy(
            src_ref=rew, dst_ref=parts_out.at[z], send_sem=z_send, recv_sem=z_recv,
            device_id=(me, lax.rem(z + o, NZ)), device_id_type=MESH,
        ).start()
        return carry

    lax.fori_loop(1, NZ, send_z, 0)
    own_part.wait()
    part = parts_out.at[pl.ds(0, NZ - 1)]
    pltpu.make_async_copy(part, part, z_recv).wait()
    pltpu.make_async_copy(part, part, z_send).wait()
    pltpu.make_async_copy(kept_out, kept_out, keep_recv).wait()

    helper = jnp.logical_or(keeps, parents)

    @pl.when(helper)
    def _():
        sent = mid.at[pl.ds(0, 24 * cap)]
        pltpu.make_async_copy(sent, sent, p1_send).wait()
        passed = pack.at[pl.ds(0, NBEAM - 1)]
        pltpu.make_async_copy(passed, passed, p2_send).wait()

    @pl.when(jnp.logical_not(helper))
    def _():
        sent = mid.at[pl.ds(0, 25 * cap)]
        pltpu.make_async_copy(sent, sent, p1_send).wait()


PARENT_AT = 8
FIRST = 12
EARLY = 16
SMEM = pl.BlockSpec(memory_space=pltpu.SMEM)
VMEM = pl.BlockSpec(memory_space=pltpu.VMEM)
HBM = pl.BlockSpec(memory_space=pl.ANY)


def tree_step(cap, *operands):
    NZ = lax.axis_size("mp")
    dma = pltpu.SemaphoreType.DMA
    return pl.pallas_call(
        functools.partial(kernel, cap),
        out_shape=(
            jax.ShapeDtypeStruct((NZ, BEAMS, HEAD), F32),
            jax.ShapeDtypeStruct((GROUPS, 2 * HEAD, HEAD), BF),
        ),
        in_specs=[SMEM, SMEM, SMEM, SMEM, VMEM, VMEM, VMEM, HBM, HBM, HBM, HBM],
        out_specs=(HBM, HBM),
        scratch_shapes=[
            pltpu.VMEM((BEAMS, HEAD, HEADS * HEAD), BF),
            pltpu.VMEM((BEAMS, 2, HEAD, HEAD), BF),
            pltpu.VMEM((BEAMS, 2, HEAD, HEAD), BF),
            pltpu.VMEM((POOL, 2, HEAD, HEAD), BF),
            pltpu.VMEM((GROUPS, HEAD, HEAD), BF),
            pltpu.VMEM((GROUPS, 2, HEAD, HEAD), BF),
            pltpu.VMEM((cap, 16, HEAD), BF),
            pltpu.VMEM((NBEAM * cap, 16, HEAD), BF),
            pltpu.VMEM((NBEAM, GROUPS, 16, HEAD), BF),
            pltpu.VMEM((GROUPS, HEAD + 16, HEAD), BF),
            pltpu.VMEM((BEAMS, HEAD), F32),
            pltpu.VMEM((16, HEAD), jnp.int32),
            pltpu.SMEM((16, HEAD), jnp.int32),
            pltpu.VMEM((POOL + BEAMS, HEADS, HEAD, HEAD), F32),
            pltpu.VMEM((HEAD, HEADS * HEAD), BF),
            pltpu.VMEM((6 * HEAD, HEAD), BF),
            pltpu.VMEM((6 * HEAD, 2 * HEAD), F32),
            pltpu.VMEM((6 * HEAD, 2 * HEAD), F32),
            pltpu.VMEM((8, 2 * HEAD), F32),
            pltpu.VMEM((8, 2 * HEAD), F32),
            pltpu.VMEM((BEAMS, HEADS, HEAD), F32),
            pltpu.VMEM((BEAMS, HEADS, HEAD), F32),
            pltpu.VMEM((BEAMS, HEADS, HEAD), F32),
            dma((5,)), dma, dma, dma, dma, dma, dma, dma, dma,
        ],
        compiler_params=pltpu.CompilerParams(
            collective_id=cap, has_side_effects=True, vmem_limit_bytes=56 << 20
        ),
        name="tree_step_%d" % cap,
    )(*operands)


def finish_kernel(parts, kept_in, rew_out, kept_out, sem):
    copies = [pltpu.make_async_copy(kept_in.at[i], kept_out.at[i], sem.at[i]) for i in range(GROUPS)]
    for copy in copies:
        copy.start()
    total = parts[0]
    for i in range(1, parts.shape[0]):
        total = total + parts[i]
    rew_out[...] = total
    for copy in copies:
        copy.wait()


def on_device(
    queries, new_kv, newest_key_value, ancestor_block_store, parent, ancestors, ancestor_count, keep_list, w_reward
):
    device = jnp.arange(NBEAM, dtype=jnp.int32)
    gives_p = jnp.sum((parent[:, None] // BEAMS == device).astype(jnp.int32), axis=0)
    gives_k = jnp.sum((keep_list[:, None] // BEAMS == device).astype(jnp.int32), axis=0)
    even = jnp.max(jnp.maximum(gives_p, 2 * gives_k)) <= 2 * GROUPS
    parts, kept = lax.cond(
        even,
        functools.partial(tree_step, GROUPS),
        functools.partial(tree_step, BEAMS),
        parent, keep_list, ancestors.T, ancestor_count, parent.reshape(4, HEAD), keep_list.reshape(2, HEAD),
        w_reward.reshape(HEADS, HEAD), queries, new_kv, newest_key_value, ancestor_block_store,
    )
    reward, kept = pl.pallas_call(
        finish_kernel,
        out_shape=(
            jax.ShapeDtypeStruct((BEAMS, HEAD), F32),
            jax.ShapeDtypeStruct((GROUPS, 2 * HEAD, HEAD), BF),
        ),
        in_specs=[VMEM, HBM],
        out_specs=(VMEM, HBM),
        scratch_shapes=[pltpu.SemaphoreType.DMA((GROUPS,))],
        name="finish",
    )(parts, kept)
    return reward, kept.reshape(GROUPS, 2, HEAD, HEAD)


def solution(mesh):
    placed = (
        P("beam", None, "mp"),
        P("beam", None, None, "mp"),
        P("beam", None, None, "mp"),
        P("beam", None, None, "mp"),
        P(),
        P("beam", None),
        P("beam"),
        P(),
        P("mp"),
    )
    return jax.shard_map(
        on_device,
        mesh=mesh,
        in_specs=placed,
        out_specs=(P("beam", None), P("beam", None, None, "mp")),
        check_vma=False,
    )
```

```python
import functools

import jax
import jax.numpy as jnp
from jax import lax
from jax.experimental import pallas as pl
from jax.experimental.pallas import tpu as pltpu
from jax.sharding import PartitionSpec as P

F32 = jnp.float32
BF = jnp.bfloat16
HEAD = 128
NBEAM = 32
BEAMS = 16
GROUPS = 8
POOL = 12
ANC = 5
HEADS = 8
SCALE2 = HEAD**-0.5 * 1.4426950408889634
NEG = -1e30
NT = (((1,), (1,)), ((), ()))
TN = (((0,), (0,)), ((), ()))
MESH = pl.DeviceIdType.MESH


def head_select(rows):
    r = lax.broadcasted_iota(jnp.int32, (rows, HEADS * HEAD), 0)
    h = lax.broadcasted_iota(jnp.int32, (rows, HEADS * HEAD), 1) // HEAD
    return jnp.where(r % HEADS == h, 1.0, 0.0).astype(BF)


def fold8(x):
    return jnp.sum(x.reshape(16, 8, HEAD), axis=0)


def value_terms(w16, anc, own, vwb, wrep):
    wrep[...] = lax.dot_general(w16, head_select(16), TN, preferred_element_type=F32).astype(BF)

    def put(block, at):
        r = jnp.dot(block, wrep[...], preferred_element_type=F32)
        for h in range(HEADS):
            vwb[at, h] = r[:, h * HEAD : (h + 1) * HEAD]

    def pool(i, carry):
        for u in range(4):
            put(anc[4 * i + u, 1], 4 * i + u)
        return carry

    def new(i, carry):
        for u in range(4):
            put(own[4 * i + u, 1], POOL + 4 * i + u)
        return carry

    lax.fori_loop(0, POOL // 4, pool, 0)
    lax.fori_loop(0, BEAMS // 4, new, 0)


def two_heads(q, b, hp):
    lo = hp * 2 * HEAD
    return jnp.concatenate([q[b, :, lo : lo + HEAD], q[b, :, lo + HEAD : lo + 2 * HEAD]], axis=0)


def attend_local(slot_block, slot_live, q, anc, own, vwb, kb, s0, s1, m0, m1, stm, stn, std, lo, hi):
    row = lax.broadcasted_iota(jnp.int32, (HEAD, 2 * HEAD), 0)
    col = lax.broadcasted_iota(jnp.int32, (HEAD, 2 * HEAD), 1) % HEAD
    causal = row <= col
    own_at = ANC * HEAD

    def gather(b):
        for a in range(ANC):
            kb[a * HEAD : (a + 1) * HEAD, :] = anc[slot_block(b, a), 0]
        kb[own_at : own_at + HEAD, :] = own[b, 0]

    def scores(b, hp, s, m):
        r = lax.dot_general(kb[...], two_heads(q, b, hp), NT, preferred_element_type=F32)
        ra = r[:own_at]
        ro = jnp.where(causal, r[own_at:], NEG)
        s[0:own_at, :] = ra
        s[own_at : own_at + HEAD, :] = ro
        mm = jnp.maximum(jnp.max(ra, axis=0, keepdims=True), jnp.max(ro, axis=0, keepdims=True))
        m[0:1, :] = mm * SCALE2

    def weigh(b, hp, s, m):
        for j in range(2):
            h = 2 * hp + j
            mj = m[0:1, j * HEAD : (j + 1) * HEAD]
            num = jnp.zeros((8, HEAD), F32)
            den = jnp.zeros((8, HEAD), F32)
            for a in range(ANC + 1):
                v = slot_block(b, a) if a < ANC else POOL + b
                e = jnp.exp2(s[a * HEAD : (a + 1) * HEAD, j * HEAD : (j + 1) * HEAD] * SCALE2 - mj)
                d_part = fold8(e)
                n_part = fold8(e * vwb[v, h])
                if 0 < a < ANC:
                    live = slot_live(b, a)
                    d_part = d_part * live
                    n_part = n_part * live
                num = num + n_part
                den = den + d_part
            stm[b, h : h + 1, :] = mj
            stn[b, h : h + 1, :] = jnp.sum(num, axis=0, keepdims=True)
            std[b, h : h + 1, :] = jnp.sum(den, axis=0, keepdims=True)

    gather(lo)
    scores(lo, 0, s0, m0)

    def body(b, carry):
        later = jnp.minimum(b + 1, hi - 1)
        scores(b, 1, s1, m1)
        weigh(b, 0, s0, m0)
        scores(b, 2, s0, m0)
        weigh(b, 1, s1, m1)
        scores(b, 3, s1, m1)
        weigh(b, 2, s0, m0)
        gather(later)
        scores(later, 0, s0, m0)
        weigh(b, 3, s1, m1)
        return carry

    lax.fori_loop(lo, hi, body, 0)


def attend_parent(q, pbuf, stm, stn, std, rew):
    pick = head_select(16)

    def beam(g, b, terms):
        scores, tops = [], []
        for hp in range(4):
            s = lax.dot_general(pbuf[g, 0:HEAD, :], two_heads(q, b, hp), NT, preferred_element_type=F32)
            top = jnp.max(s, axis=0, keepdims=True)
            for j in range(2):
                scores.append(s[:, j * HEAD : (j + 1) * HEAD])
                tops.append(top[:, j * HEAD : (j + 1) * HEAD])
        ma = stm[b]
        m = jnp.maximum(ma, jnp.concatenate(tops, axis=0) * SCALE2)
        f = jnp.exp2(ma - m)
        dens, nums = [], []
        for h in range(HEADS):
            e = jnp.exp2(scores[h] * SCALE2 - m[h : h + 1])
            dens.append(jnp.sum(fold8(e), axis=0, keepdims=True))
            nums.append(jnp.sum(fold8(e * terms[:, h * HEAD : (h + 1) * HEAD]), axis=0, keepdims=True))
        den = jnp.concatenate(dens, axis=0) + std[b] * f
        num = jnp.concatenate(nums, axis=0) + stn[b] * f
        rew[pl.ds(b, 1), :] = jnp.sum(num / den, axis=0, keepdims=True)

    def groups(i, carry):
        for u in range(4):
            g = 4 * i + u
            terms = lax.dot_general(pbuf[g, HEAD : HEAD + 16, :], pick, TN, preferred_element_type=F32)
            for c in range(2):
                beam(g, 2 * g + c, terms)
        return carry

    lax.fori_loop(0, GROUPS // 4, groups, 0)


def parent_helper(u):
    y = u // 2
    chip = jnp.where(u < 8, 4 * y + y % 2 + 2 * (u % 2), 6)
    return 2 * chip + 1 - (chip // 4) % 2


def keep_helper(t):
    return 2 * t + (t // 4) % 2


def ranks(rows):
    wide = [jnp.broadcast_to(r, (HEAD, HEAD)) for r in rows]
    tall = [x.T for x in wide]
    earlier = lax.broadcasted_iota(jnp.int32, (HEAD, HEAD), 0) < lax.broadcasted_iota(jnp.int32, (HEAD, HEAD), 1)
    out = []
    for j in range(len(rows)):
        same = jnp.where(jnp.logical_and(tall[j] == wide[j], earlier), 1, 0)
        for i in range(j):
            same = same + jnp.where(tall[i] == wide[j], 1, 0)
        out.append(jnp.sum(same, axis=0, keepdims=True))
    return out


def routes(me, x, children):
    rows = [x[c : c + 1, :] for c in range(x.shape[0])]
    source = [lax.shift_right_logical(r, 4) for r in rows]
    place = [lax.shift_right_logical(r, children - 1) for r in ranks(source)]
    index = [jnp.minimum(s * GROUPS + p, NBEAM * GROUPS - 1) for s, p in zip(source, place)]
    slot = lax.broadcasted_iota(jnp.int32, (GROUPS, HEAD), 0)
    lane = lax.broadcasted_iota(jnp.int32, (GROUPS, HEAD), 1)
    first = lax.rem(lane, children) == 0
    given = jnp.zeros((GROUPS, HEAD), jnp.int32)
    for r, s, p in zip(rows, source, place):
        hit = jnp.logical_and(jnp.logical_and(s == me, p == slot), first)
        given = given + jnp.where(hit, lax.rem(r, BEAMS), 0)
    return index, jnp.sum(given, axis=1, keepdims=True)


STEPS = (
    (1, 0), (0, 1), (3, 0), (0, 3), (1, 1), (3, 3), (1, 3), (3, 1),
    (2, 0), (0, 2), (2, 1), (1, 2), (2, 3), (3, 2), (2, 2), (0, 0),
)


def kernel(
    cap,
    parent, keep, ancestors, count, parent_v, keep_v, w, q_hbm, new_hbm, newest_hbm, anc_hbm,
    parts_out, kept_out,
    q, own, newest, anc, given_p, given_k, vwt, mid, pack, pbuf, rew, tab_v, tab,
    vwb, wrep, kb, s0, s1, m0, m1, stm, stn, std,
    load_sem, p1_send, p1_recv, p2_send, par_recv, keep_recv, z_send, z_recv, z_own,
):
    NZ = lax.axis_size("mp")
    me = lax.axis_index("beam")
    z = lax.axis_index("mp")
    chip = me // 2
    core = me % 2
    chip_y = chip // 4
    chip_x = chip % 4
    keeps = core == chip_y % 2
    tile_even = (chip_x + chip_y) % 2 == 0
    parents = jnp.logical_and(core != chip_y % 2, jnp.logical_or(tile_even, chip == 6))
    tile_u = jnp.where(tile_even, 2 * chip_y + (chip_x - chip_y % 2) // 2, 8)

    barrier = pltpu.get_barrier_semaphore()

    def greet(o, carry):
        pl.semaphore_signal(barrier, inc=1, device_id=(lax.rem(me + o, NBEAM), z), device_id_type=MESH)
        return carry

    def greet_z(o, carry):
        pl.semaphore_signal(barrier, inc=1, device_id=(me, lax.rem(z + o, NZ)), device_id_type=MESH)
        return carry

    loads = [
        pltpu.make_async_copy(newest_hbm, newest, load_sem.at[0]),
        pltpu.make_async_copy(new_hbm, own, load_sem.at[1]),
        pltpu.make_async_copy(anc_hbm, anc, load_sem.at[2]),
        pltpu.make_async_copy(q_hbm, q, load_sem.at[3]),
    ]
    lax.fori_loop(1, NBEAM, greet, 0)
    lax.fori_loop(1, NZ, greet_z, 0)
    for load in loads:
        load.start()

    if cap < BEAMS:
        index_p, mine_p = routes(me, parent_v[...], 2)
        index_k, mine_k = routes(me, keep_v[...], 1)
        for c in range(4):
            tab_v[c : c + 1, :] = index_p[c]
        for c in range(2):
            tab_v[4 + c : 5 + c, :] = index_k[c]
        lane = lax.broadcasted_iota(jnp.int32, (GROUPS, HEAD), 1)
        tab_v[8:16, :] = jnp.where(lane == 0, mine_p, mine_k)
        to_smem = pltpu.make_async_copy(tab_v, tab, load_sem.at[4])
        to_smem.start()
        to_smem.wait()
        loads[0].wait()
        for r in range(cap):
            given_p[r] = newest[tab[8 + r, 0], 0]
        tiles_p = given_p

        def value_block(i):
            return newest[tab[8 + i, 0], 1]

        def index_parent(d, k):
            return tab[d // 8, (d % 8) * BEAMS + 2 * k]

        def index_keep(d, k):
            return tab[4 + d // 16, (d % 16) * GROUPS + k]

    else:
        loads[0].wait()
        tiles_p = newest.at[:, 0]

        def value_block(i):
            return newest[i, 1]

        def index_parent(d, k):
            return parent[d * BEAMS + 2 * k]

        def index_keep(d, k):
            return keep[d * GROUPS + k]

    pl.semaphore_wait(barrier, NBEAM - 1 + NZ - 1)

    mine = pl.ds(me * cap, cap)

    def spread(src, peer):
        @pl.when(peer != me)
        def _():
            pltpu.make_async_remote_copy(
                src_ref=src, dst_ref=mid.at[mine], send_sem=p1_send, recv_sem=p1_recv,
                device_id=(peer, z), device_id_type=MESH,
            ).start()

        @pl.when(peer == me)
        def _():
            pltpu.make_async_copy(src, mid.at[mine], p1_recv).start()

    def spread_parent(o, carry):
        u = lax.rem(me + o, 8)
        spread(tiles_p.at[:, pl.ds(u * 16, 16), :], parent_helper(u))
        return carry

    lax.fori_loop(0, 8, spread_parent, 0)

    w16 = jnp.concatenate([w[...].astype(F32), jnp.zeros((8, HEAD), F32)], axis=0).astype(BF)

    def value_tile(i, carry):
        for u in range(4):
            r = lax.dot_general(w16, value_block(4 * i + u), NT, preferred_element_type=F32)[:8]
            top = r.astype(BF).astype(F32)
            vwt[4 * i + u] = jnp.concatenate([top, r - top], axis=0).astype(BF)
        return carry

    lax.fori_loop(0, cap // 4, value_tile, 0)
    spread(vwt, parent_helper(8))

    loads[1].wait()
    if cap < BEAMS:
        for r in range(cap):
            given_k[r] = own[tab[8 + r, 1]]
        tiles_k = given_k
    else:
        tiles_k = own

    def spread_keep(steps):
        for dx, dy in steps:
            t = ((chip_y + dy) % 4) * 4 + (chip_x + dx) % 4
            spread(tiles_k.at[:, t // 8, pl.ds((t % 8) * 16, 16), :], keep_helper(t))

    spread_keep(STEPS[:EARLY])

    def hand_on(index, dst, recv):
        pltpu.make_async_copy(mid, mid, p1_recv).wait()

        def to(o, carry):
            dests = [lax.rem(me + 4 * o + i, NBEAM) for i in range(4)]
            picked = [[mid[index(d, k)] for k in range(GROUPS)] for d in dests]
            for d, blocks in zip(dests, picked):
                for k in range(GROUPS):
                    pack[d, k] = blocks[k]
            for d in dests:
                @pl.when(d != me)
                def _():
                    pltpu.make_async_remote_copy(
                        src_ref=pack.at[d], dst_ref=dst, send_sem=p2_send, recv_sem=recv,
                        device_id=(d, z), device_id_type=MESH,
                    ).start()

                @pl.when(d == me)
                def _():
                    pltpu.make_async_copy(pack.at[d], dst, recv).start()

            return carry

        lax.fori_loop(0, NBEAM // 4, to, 0)

    loads[2].wait()
    value_terms(w16, anc, own, vwb, wrep)

    loads[3].wait()

    def slot_block(b, a):
        return lax.rem(jnp.where(a < count[b], ancestors[a, b], ancestors[0, b]), POOL)

    def slot_live(b, a):
        return jnp.where(a < count[b], 1.0, 0.0)

    local = functools.partial(
        attend_local, slot_block, slot_live, q, anc, own, vwb, kb, s0, s1, m0, m1, stm, stn, std
    )
    spread_keep(STEPS[EARLY:])
    local(0, PARENT_AT)

    @pl.when(parents)
    def _():
        rows = pl.ds(tile_u * 16, 16)
        hand_on(index_parent, pbuf.at[:, rows, :], par_recv)

    local(PARENT_AT, FIRST)

    @pl.when(keeps)
    def _():
        rows = pl.ds(chip * 16, 16)
        hand_on(index_keep, kept_out.at[:, rows, :], keep_recv)

    if FIRST < BEAMS:
        local(FIRST, BEAMS)
    pltpu.make_async_copy(pbuf, pbuf, par_recv).wait()
    attend_parent(q, pbuf, stm, stn, std, rew)

    own_part = pltpu.make_async_copy(rew, parts_out.at[z], z_own)
    own_part.start()

    def send_z(o, carry):
        pltpu.make_async_remote_copy(
            src_ref=rew, dst_ref=parts_out.at[z], send_sem=z_send, recv_sem=z_recv,
            device_id=(me, lax.rem(z + o, NZ)), device_id_type=MESH,
        ).start()
        return carry

    lax.fori_loop(1, NZ, send_z, 0)
    own_part.wait()
    part = parts_out.at[pl.ds(0, NZ - 1)]
    pltpu.make_async_copy(part, part, z_recv).wait()
    pltpu.make_async_copy(part, part, z_send).wait()
    pltpu.make_async_copy(kept_out, kept_out, keep_recv).wait()

    helper = jnp.logical_or(keeps, parents)

    @pl.when(helper)
    def _():
        sent = mid.at[pl.ds(0, 24 * cap)]
        pltpu.make_async_copy(sent, sent, p1_send).wait()
        passed = pack.at[pl.ds(0, NBEAM - 1)]
        pltpu.make_async_copy(passed, passed, p2_send).wait()

    @pl.when(jnp.logical_not(helper))
    def _():
        sent = mid.at[pl.ds(0, 25 * cap)]
        pltpu.make_async_copy(sent, sent, p1_send).wait()


PARENT_AT = 8
FIRST = 12
EARLY = 16
SMEM = pl.BlockSpec(memory_space=pltpu.SMEM)
VMEM = pl.BlockSpec(memory_space=pltpu.VMEM)
HBM = pl.BlockSpec(memory_space=pl.ANY)


def tree_step(cap, *operands):
    NZ = lax.axis_size("mp")
    dma = pltpu.SemaphoreType.DMA
    return pl.pallas_call(
        functools.partial(kernel, cap),
        out_shape=(
            jax.ShapeDtypeStruct((NZ, BEAMS, HEAD), F32),
            jax.ShapeDtypeStruct((GROUPS, 2 * HEAD, HEAD), BF),
        ),
        in_specs=[SMEM, SMEM, SMEM, SMEM, VMEM, VMEM, VMEM, HBM, HBM, HBM, HBM],
        out_specs=(HBM, HBM),
        scratch_shapes=[
            pltpu.VMEM((BEAMS, HEAD, HEADS * HEAD), BF),
            pltpu.VMEM((BEAMS, 2, HEAD, HEAD), BF),
            pltpu.VMEM((BEAMS, 2, HEAD, HEAD), BF),
            pltpu.VMEM((POOL, 2, HEAD, HEAD), BF),
            pltpu.VMEM((GROUPS, HEAD, HEAD), BF),
            pltpu.VMEM((GROUPS, 2, HEAD, HEAD), BF),
            pltpu.VMEM((cap, 16, HEAD), BF),
            pltpu.VMEM((NBEAM * cap, 16, HEAD), BF),
            pltpu.VMEM((NBEAM, GROUPS, 16, HEAD), BF),
            pltpu.VMEM((GROUPS, HEAD + 16, HEAD), BF),
            pltpu.VMEM((BEAMS, HEAD), F32),
            pltpu.VMEM((16, HEAD), jnp.int32),
            pltpu.SMEM((16, HEAD), jnp.int32),
            pltpu.VMEM((POOL + BEAMS, HEADS, HEAD, HEAD), F32),
            pltpu.VMEM((HEAD, HEADS * HEAD), BF),
            pltpu.VMEM((6 * HEAD, HEAD), BF),
            pltpu.VMEM((6 * HEAD, 2 * HEAD), F32),
            pltpu.VMEM((6 * HEAD, 2 * HEAD), F32),
            pltpu.VMEM((8, 2 * HEAD), F32),
            pltpu.VMEM((8, 2 * HEAD), F32),
            pltpu.VMEM((BEAMS, HEADS, HEAD), F32),
            pltpu.VMEM((BEAMS, HEADS, HEAD), F32),
            pltpu.VMEM((BEAMS, HEADS, HEAD), F32),
            dma((5,)), dma, dma, dma, dma, dma, dma, dma, dma,
        ],
        compiler_params=pltpu.CompilerParams(
            collective_id=cap, has_side_effects=True, vmem_limit_bytes=56 << 20
        ),
        name="tree_step_%d" % cap,
    )(*operands)


def most_kernel(parent_v, keep_v, most):
    device = lax.broadcasted_iota(jnp.int32, (NBEAM, HEAD), 0)

    def gives(x):
        total = jnp.zeros((NBEAM, HEAD), jnp.int32)
        for c in range(x.shape[0]):
            total = total + jnp.where(lax.shift_right_logical(x[c : c + 1, :], 4) == device, 1, 0)
        return jnp.sum(total, axis=1, keepdims=True)

    most[0] = jnp.max(jnp.maximum(gives(parent_v[...]), 2 * gives(keep_v[...])))


def finish_kernel(parts, kept_in, rew_out, kept_out, sem):
    copies = [pltpu.make_async_copy(kept_in.at[i], kept_out.at[i], sem.at[i]) for i in range(GROUPS)]
    for copy in copies:
        copy.start()
    total = parts[0]
    for i in range(1, parts.shape[0]):
        total = total + parts[i]
    rew_out[...] = total
    for copy in copies:
        copy.wait()


def on_device(
    queries, new_kv, newest_key_value, ancestor_block_store, parent, ancestors, ancestor_count, keep_list, w_reward
):
    most = pl.pallas_call(
        most_kernel,
        out_shape=jax.ShapeDtypeStruct((1,), jnp.int32),
        in_specs=[VMEM, VMEM],
        out_specs=SMEM,
        name="most",
    )(parent.reshape(4, HEAD), keep_list.reshape(2, HEAD))
    even = most[0] <= 2 * GROUPS
    parts, kept = lax.cond(
        even,
        functools.partial(tree_step, GROUPS),
        functools.partial(tree_step, BEAMS),
        parent, keep_list, ancestors.T, ancestor_count, parent.reshape(4, HEAD), keep_list.reshape(2, HEAD),
        w_reward.reshape(HEADS, HEAD), queries, new_kv, newest_key_value, ancestor_block_store,
    )
    reward, kept = pl.pallas_call(
        finish_kernel,
        out_shape=(
            jax.ShapeDtypeStruct((BEAMS, HEAD), F32),
            jax.ShapeDtypeStruct((GROUPS, 2 * HEAD, HEAD), BF),
        ),
        in_specs=[VMEM, HBM],
        out_specs=(VMEM, HBM),
        scratch_shapes=[pltpu.SemaphoreType.DMA((GROUPS,))],
        name="finish",
    )(parts, kept)
    return reward, kept.reshape(GROUPS, 2, HEAD, HEAD)


def solution(mesh):
    placed = (
        P("beam", None, "mp"),
        P("beam", None, None, "mp"),
        P("beam", None, None, "mp"),
        P("beam", None, None, "mp"),
        P(),
        P("beam", None),
        P("beam"),
        P(),
        P("mp"),
    )
    return jax.shard_map(
        on_device,
        mesh=mesh,
        in_specs=placed,
        out_specs=(P("beam", None), P("beam", None, None, "mp")),
        check_vma=False,
    )
```
